32 devices in a mesh: space: 4 (over y, core), test: 2 (over x), trial: 4 (over z).
Axes of the slice: x: 2, y: 2, z: 4, core: 2. Of those that a mesh axis runs over, the one named last changes fastest.
Arguments:
- test_modes: bfloat16 [3, 128, 16, 8, 128], P(None, 'test', 'space'), may hold values from -6 to 6
- trial_modes: bfloat16 [3, 128, 16, 8, 128], P(None, 'trial', 'space'), may hold values from -6 to 6
- volumes: float32 [16, 8, 128], P('space'), may hold values from 0.25 to 4
Outputs:
- tensor: float32 [128, 128, 128], P('space', 'test', 'trial')
The draws below stay inside these ranges and needn't reach their ends.
All inputs are finite; a program needn't handle non-finite values.
Results may differ from the reference program's by a relative error of at most 0.0051.
Values may be sent and summed in bfloat16 or wider, within the bound.
A program may use at most 64 MiB of HBM per device.

```python
import math
import jax
import jax.numpy as jnp
from jax import lax

R = 128
NY = 8
NZ = 128
NX = 16


def levels(rng, extent, shards, low, high):
    def one(dim, blocks):
        heights = jax.random.uniform(jax.random.fold_in(jax.random.fold_in(rng, 6), dim), (blocks,), jnp.float32, low / len(shards), high / len(shards))
        return jnp.repeat(jnp.exp(heights), extent[dim] // blocks).reshape((-1,) + (1,) * (len(extent) - dim - 1))

    factor_of = one(*shards[0])
    for cut in shards[1:]:
        factor_of = factor_of * one(*cut)
    return factor_of


def gaussian(stream_key, shape, width, most, cuts=(), dtype=jnp.bfloat16):
    values = width * jax.random.normal(stream_key, shape, jnp.float32)
    if cuts:
        values = values * levels(stream_key, shape, cuts, -0.22, 0.18)
    return jnp.clip(values, -most, most).astype(dtype)


def setup_inputs(seed: int = 0) -> dict:
    key_list = jax.random.split(jax.random.key(seed), 4)
    return {
        "test_modes": gaussian(key_list[0], (3, R, NX, NY, NZ), 1.0, 6.0, ((1, 2), (2, 4))),
        "trial_modes": gaussian(key_list[1], (3, R, NX, NY, NZ), 1.0, 6.0, ((1, 4), (2, 4))),
        "volumes": jnp.clip(jnp.exp(math.log(4.0) - 2.7725887 * jax.random.uniform(key_list[2], (NX, NY, NZ), jnp.float32) ** levels(key_list[2], (NX, NY, NZ), ((0, 4),), -0.2, 0.2)), 0.25, 4.0),
    }


def derivatives(padded):
    field = padded.astype(jnp.float32)
    along_x = (field[:, :, 2:] - field[:, :, :-2]) * 0.5
    center = field[:, :, 1:-1]
    wide_y = jnp.pad(center, ((0, 0), (0, 0), (0, 0), (1, 1), (0, 0)))
    along_y = (wide_y[:, :, :, 2:] - wide_y[:, :, :, :-2]) * 0.5
    wide_z = jnp.pad(center, ((0, 0), (0, 0), (0, 0), (0, 0), (1, 1)))
    along_z = (wide_z[:, :, :, :, 2:] - wide_z[:, :, :, :, :-2]) * 0.5
    return jnp.stack([along_x, along_y, along_z], axis=1).astype(jnp.bfloat16)

def reference(test_modes, trial_modes, volumes):
    cell_count = NX * NY * NZ
    padded = jnp.pad(trial_modes, ((0, 0), (0, 0), (1, 1), (0, 0), (0, 0)))
    gradients = derivatives(padded)
    weighted = (test_modes.astype(jnp.float32) * volumes).astype(jnp.bfloat16)

    def advance(position, running):
        plane = (position // NY).astype(jnp.int32)
        row = (position % NY).astype(jnp.int32)
        trial_block = lax.dynamic_index_in_dim(lax.dynamic_index_in_dim(trial_modes, plane, 2, False), row, 2, False).astype(jnp.float32)
        grad_block = lax.dynamic_index_in_dim(lax.dynamic_index_in_dim(gradients, plane, 3, False), row, 3, False).astype(jnp.float32)
        test_block = lax.dynamic_index_in_dim(lax.dynamic_index_in_dim(weighted, plane, 2, False), row, 2, False).astype(jnp.float32)
        convected = jnp.einsum('bjc,abkc->ajkc', trial_block, grad_block).astype(jnp.bfloat16)
        convected = lax.optimization_barrier(convected).astype(jnp.float32)
        return running + jnp.einsum('aic,ajkc->jik', test_block, convected)
    running = jnp.zeros((R, R, R), jnp.float32)
    running = lax.fori_loop(0, NX * NY, advance, running)
    return running * (1.0 / (4.0 * math.sqrt(cell_count)))
```

```python
import functools
import math

import jax
import jax.numpy as jnp
from jax import lax
from jax.experimental import pallas as pl
from jax.experimental.pallas import tpu as pltpu
from jax.sharding import PartitionSpec as P

GROUP = 8
MIXED = jnp.float32


def slope(later, earlier):
    return (later.astype(jnp.float32) - earlier.astype(jnp.float32)) * 0.5


def gradients_of_plane(before, here, after):
    rows, parts, modes, lanes = here.shape
    none = jnp.zeros((1, parts, modes, lanes), here.dtype)
    along_x = slope(after, before)
    along_y = slope(
        jnp.concatenate([here[1:], none], axis=0), jnp.concatenate([none, here[:-1]], axis=0)
    )
    wide = here.astype(jnp.float32).reshape(rows * parts * modes, lanes)
    lane = lax.broadcasted_iota(jnp.int32, wide.shape, 1)
    following = jnp.where(lane == lanes - 1, 0.0, pltpu.roll(wide, lanes - 1, 1))
    previous = jnp.where(lane == 0, 0.0, pltpu.roll(wide, 1, 1))
    along_z = ((following - previous) * 0.5).reshape(here.shape)
    return along_x, along_y, along_z


def pair_rows(weighted_ref, grad_ref, plane, first_row, rows, first_mode):
    columns = []
    for row in range(rows):
        grads = [[grad_ref[plane, first_row + row, a, b] for b in range(3)] for a in range(3)]
        per_mode = []
        for mode in range(GROUP):
            w = [
                jnp.broadcast_to(
                    weighted_ref[plane, first_row + row, a, pl.ds(first_mode + mode, 1), :],
                    grads[0][0].shape,
                ).astype(MIXED)
                for a in range(3)
            ]
            per_mode.append(
                [
                    (w[0] * grads[0][b] + w[1] * grads[1][b] + w[2] * grads[2][b]).astype(jnp.bfloat16)
                    for b in range(3)
                ]
            )
        for b in range(3):
            columns.append(jnp.concatenate([m[b] for m in per_mode], axis=0))
    return jnp.concatenate(columns, axis=1)


def kernel(padded_ref, all_ref, weighted_ref, out_ref, grad_ref, total_ref):
    planes, rows_each = all_ref.shape[0], all_ref.shape[1]
    modes = padded_ref.shape[3]
    tests = weighted_ref.shape[3]

    @pl.loop(0, planes)
    def _(plane):
        found = gradients_of_plane(padded_ref[plane], padded_ref[plane + 1], padded_ref[plane + 2])
        for b in range(3):
            grad_ref[plane, :, :, b] = found[b].astype(jnp.bfloat16).astype(MIXED)

    total_ref[...] = jnp.zeros_like(total_ref)
    pairs = rows_each // 2
    unroll = 4
    span = GROUP * unroll

    @pl.loop(0, planes * pairs * (tests // span))
    def _(step):
        part = step % (tests // span)
        place = step // (tests // span)
        plane, row = place // pairs, (place % pairs) * 2
        trial = jnp.concatenate(
            [all_ref[plane, row + r, b] for r in range(2) for b in range(3)], axis=1
        )
        for u in range(unroll):
            first = part * span + u * GROUP
            lhs = pair_rows(weighted_ref, grad_ref, plane, row, 2, first)
            where = pl.ds(pl.multiple_of(first * modes, GROUP * modes), GROUP * modes)
            total_ref[where, :] += lax.dot_general(
                lhs, trial, (((1,), (1,)), ((), ())), preferred_element_type=jnp.float32
            )

    out_ref[...] = total_ref[...].T


def shards(test_modes, trial_modes, volumes):
    cell_count = trial_modes.shape[2] * trial_modes.shape[3] * trial_modes.shape[4]
    count = lax.axis_size("space")
    factor = 1.0 / (4.0 * math.sqrt(cell_count * count))
    order = (2, 3, 0, 1, 4)
    own = jnp.transpose(trial_modes, order)
    weighted = jnp.transpose(
        (test_modes.astype(jnp.float32) * volumes).astype(jnp.bfloat16), order
    ).astype(jnp.float32)
    ends = count - 1
    padded = jnp.concatenate(
        [
            lax.ppermute(own[-1:], "space", [(i, i + 1) for i in range(ends)]),
            own,
            lax.ppermute(own[:1], "space", [(i + 1, i) for i in range(ends)]),
        ],
        axis=0,
    )
    every = lax.all_gather(own, "trial", axis=3, tiled=True)
    planes, rows_each, _, modes, lanes = own.shape
    tests = weighted.shape[3]
    total = pl.pallas_call(
        kernel,
        out_shape=jax.ShapeDtypeStruct((every.shape[3], tests * modes), jnp.float32),
        in_specs=[pl.BlockSpec(memory_space=pltpu.VMEM)] * 3,
        out_specs=pl.BlockSpec(memory_space=pltpu.VMEM),
        scratch_shapes=[
            pltpu.VMEM((planes, rows_each, 3, 3, modes, lanes), MIXED),
            pltpu.VMEM((tests * modes, every.shape[3]), jnp.float32),
        ],
        compiler_params=pltpu.CompilerParams(vmem_limit_bytes=48 * 2**20),
    )(padded, every, weighted)
    mine = lax.psum_scatter(total, "space", scatter_dimension=0, tiled=True) * factor
    return mine.reshape(mine.shape[0], tests, modes)


def solution(mesh):
    return jax.shard_map(
        shards,
        mesh=mesh,
        in_specs=(
            P(None, "test", "space", None, None),
            P(None, "trial", "space", None, None),
            P("space", None, None),
        ),
        out_specs=P("space", "test", "trial"),
        check_vma=False,
    )
```

```python
import functools
import math

import jax
import jax.numpy as jnp
from jax import lax
from jax.experimental import pallas as pl
from jax.experimental.pallas import tpu as pltpu
from jax.sharding import PartitionSpec as P

GROUP = 8
MIXED = jnp.float32
MESH = pl.DeviceIdType.MESH


def slope(later, earlier):
    return (later.astype(jnp.float32) - earlier.astype(jnp.float32)) * 0.5


def gradients_of_plane(before, here, after):
    rows, parts, modes, lanes = here.shape
    none = jnp.zeros((1, parts, modes, lanes), here.dtype)
    along_x = slope(after, before)
    along_y = slope(
        jnp.concatenate([here[1:], none], axis=0), jnp.concatenate([none, here[:-1]], axis=0)
    )
    wide = here.astype(jnp.float32).reshape(rows * parts * modes, lanes)
    lane = lax.broadcasted_iota(jnp.int32, wide.shape, 1)
    following = jnp.where(lane == lanes - 1, 0.0, pltpu.roll(wide, lanes - 1, 1))
    previous = jnp.where(lane == 0, 0.0, pltpu.roll(wide, 1, 1))
    along_z = ((following - previous) * 0.5).reshape(here.shape)
    return along_x, along_y, along_z


def pair_rows(weighted_ref, grad_ref, plane, first_row, rows, first_mode):
    columns = []
    for row in range(rows):
        grads = [[grad_ref[plane, first_row + row, a, b] for b in range(3)] for a in range(3)]
        per_mode = []
        for mode in range(GROUP):
            w = [
                jnp.broadcast_to(
                    weighted_ref[plane, first_row + row, a, pl.ds(first_mode + mode, 1), :],
                    grads[0][0].shape,
                ).astype(MIXED)
                for a in range(3)
            ]
            per_mode.append(
                [
                    (w[0] * grads[0][b] + w[1] * grads[1][b] + w[2] * grads[2][b]).astype(jnp.bfloat16)
                    for b in range(3)
                ]
            )
        for b in range(3):
            columns.append(jnp.concatenate([m[b] for m in per_mode], axis=0))
    return jnp.concatenate(columns, axis=1)


def kernel(
    factor, own_ref, test_ref, out_ref,
    padded_ref, all_ref, weighted_ref, grad_ref, total_ref, turned_ref, send_ref, got_ref,
    halo_send, halo_recv, right_send, left_send, line_recv, cross_send, cross_recv, sum_send, sum_recv,
):
    planes, rows_each, _, modes, lanes = own_ref.shape
    tests = weighted_ref.shape[3]
    s, t, z = lax.axis_index("space"), lax.axis_index("test"), lax.axis_index("trial")
    ns, nt, nz = lax.axis_size("space"), lax.axis_size("test"), lax.axis_size("trial")
    share = rows_each // nt
    pairs = rows_each // 2
    unroll = 4
    span = GROUP * unroll
    parts = tests // span
    every = out_ref.shape[0] * ns
    piece = out_ref.shape[0]

    def block(plane, source, part):
        return all_ref.at[plane, source, pl.ds(part * share, share)]

    def along_line(plane, source, target, sems):
        return pltpu.make_async_remote_copy(
            block(plane, source, t), block(plane, source, t),
            sems.at[plane, source], line_recv.at[plane, source],
            device_id=(s, t, target), device_id_type=MESH,
        )

    def to_right(plane, source):
        return along_line(plane, source, z + 1, right_send)

    def to_left(plane, source):
        return along_line(plane, source, z - 1, left_send)

    def across(plane, source, sender, target):
        return pltpu.make_async_remote_copy(
            block(plane, source, sender), block(plane, source, sender),
            cross_send.at[plane, source, target], cross_recv.at[plane, source, sender],
            device_id=(s, target, z), device_id_type=MESH,
        )

    def halo(side):
        return pltpu.make_async_remote_copy(
            padded_ref.at[planes if side == 0 else 1], padded_ref.at[0 if side == 0 else planes + 1],
            halo_send.at[side], halo_recv.at[side],
            device_id=(s + 1 if side == 0 else s - 1, t, z), device_id_type=MESH,
        )

    def partial_to(part, peer):
        return pltpu.make_async_remote_copy(
            send_ref.at[part, peer], got_ref.at[part, s],
            sum_send.at[part, peer], sum_recv.at[part, s],
            device_id=(peer, t, z), device_id_type=MESH,
        )

    def partial_from(part, peer):
        return pltpu.make_async_remote_copy(
            send_ref.at[part, peer], got_ref.at[part, peer],
            sum_send.at[part, peer], sum_recv.at[part, peer],
            device_id=(peer, t, z), device_id_type=MESH,
        )

    barrier = pltpu.get_barrier_semaphore()

    @pl.loop(1, ns)
    def _(d):
        pl.semaphore_signal(barrier, inc=1, device_id=(lax.rem(s + d, ns), t, z), device_id_type=MESH)

    for d in range(1, nt):
        pl.semaphore_signal(barrier, inc=1, device_id=(s, lax.rem(t + d, nt), z), device_id_type=MESH)

    @pl.when(z > 0)
    def _():
        pl.semaphore_signal(barrier, inc=1, device_id=(s, t, z - 1), device_id_type=MESH)

    @pl.when(z < nz - 1)
    def _():
        pl.semaphore_signal(barrier, inc=1, device_id=(s, t, z + 1), device_id_type=MESH)

    @pl.loop(0, planes)
    def _(plane):
        here = own_ref[plane]
        padded_ref[plane + 1] = here
        all_ref[plane, z] = here

    sides = jnp.where(z > 0, 1, 0) + jnp.where(z < nz - 1, 1, 0)
    pl.semaphore_wait(barrier, ns - 1 + nt - 1 + sides)

    def send_own(plane):
        @pl.when(z < nz - 1)
        def _():
            to_right(plane, z).start()

        @pl.when(z > 0)
        def _():
            to_left(plane, z).start()

    def pass_on(plane, hop):
        before, after = z - hop, z + hop

        @pl.when(before >= 0)
        def _():
            to_right(plane, before).wait_recv()

            @pl.when(z < nz - 1)
            def _():
                to_right(plane, before).start()

            for d in range(1, nt):
                across(plane, before, t, lax.rem(t + d, nt)).start()

        @pl.when(after < nz)
        def _():
            to_left(plane, after).wait_recv()

            @pl.when(z > 0)
            def _():
                to_left(plane, after).start()

            for d in range(1, nt):
                across(plane, after, t, lax.rem(t + d, nt)).start()

    def slot(plane, hop):
        @pl.when((hop == 0) & (plane + 1 < planes))
        def _():
            send_own(plane + 1)

        @pl.when(hop > 0)
        def _():
            pass_on(plane, hop)

    def wait_across(plane):
        for d in range(1, nz):
            source = lax.rem(z + d, nz)
            for e in range(1, nt):
                across(plane, source, lax.rem(t + e, nt), t).wait_recv()

    send_own(0)

    @pl.when(s < ns - 1)
    def _():
        halo(0).start()

    @pl.when(s > 0)
    def _():
        halo(1).start()

    slot(0, 0)

    @pl.when(s == 0)
    def _():
        padded_ref[0] = jnp.zeros(padded_ref.shape[1:], padded_ref.dtype)

    @pl.when(s == ns - 1)
    def _():
        padded_ref[planes + 1] = jnp.zeros(padded_ref.shape[1:], padded_ref.dtype)

    @pl.loop(0, planes)
    def _(plane):
        weighted_ref[plane] = test_ref[plane].astype(jnp.float32)

    total_ref[...] = jnp.zeros_like(total_ref)
    for hop in range(1, nz):
        slot(0, hop)

    @pl.when(s > 0)
    def _():
        halo(0).wait_recv()

    @pl.when(s < ns - 1)
    def _():
        halo(1).wait_recv()

    @pl.loop(0, planes)
    def _(plane):
        found = gradients_of_plane(padded_ref[plane], padded_ref[plane + 1], padded_ref[plane + 2])
        for b in range(3):
            grad_ref[plane, :, :, b] = found[b].astype(jnp.bfloat16).astype(MIXED)

    def flush(part):
        rows = span * modes
        value = total_ref[pl.ds(pl.multiple_of(part * rows, rows), rows), :].T
        for peer in range(ns):
            turned_ref[part, peer] = value[peer * piece : (peer + 1) * piece]
            send_ref[part, peer] = value[peer * piece : (peer + 1) * piece].astype(jnp.bfloat16)

        @pl.loop(1, ns)
        def _(d):
            partial_to(part, lax.rem(s + d, ns)).start()

    @pl.loop(0, planes * pairs * parts)
    def _(step):
        plane, m = step // (pairs * parts), step % (pairs * parts)
        last = plane == planes - 1
        q = jnp.where(last, m % pairs, m // parts)
        part = jnp.where(last, m // pairs, m % parts)
        row = lax.rem(t * share + q * 2, rows_each)

        @pl.when(m == jnp.where(last, pairs // nt, pairs // nt * parts))
        def _():
            wait_across(plane)

        trial = jnp.concatenate(
            [
                jnp.concatenate([all_ref[plane, source, row + r, b] for source in range(nz)], axis=0)
                for r in range(2)
                for b in range(3)
            ],
            axis=1,
        )
        for u in range(unroll):
            first = part * span + u * GROUP
            lhs = pair_rows(weighted_ref, grad_ref, plane, row, 2, first)
            where = pl.ds(pl.multiple_of(first * modes, GROUP * modes), GROUP * modes)
            total_ref[where, :] += lax.dot_general(
                lhs, trial, (((1,), (1,)), ((), ())), preferred_element_type=jnp.float32
            )

        @pl.when((plane + 1 < planes) & (m % parts == parts - 1))
        def _():
            @pl.loop(m // parts * nz // pairs, (m // parts + 1) * nz // pairs)
            def _(hop):
                slot(plane + 1, hop)

        @pl.when(last & (m % pairs == pairs - 1))
        def _():
            flush(part)

    width = span * modes
    for part in range(parts):
        @pl.loop(1, ns)
        def _(d):
            peer = lax.rem(s + d, ns)
            partial_from(part, peer).wait_recv()
            turned_ref[part, s] += got_ref[part, peer].astype(jnp.float32)

        out_ref[:, part * width : (part + 1) * width] = turned_ref[part, s] * factor

    @pl.loop(0, planes)
    def _(plane):
        @pl.loop(0, nz)
        def _(source):
            @pl.when((source <= z) & (z < nz - 1))
            def _():
                to_right(plane, source).wait_send()

            @pl.when((source >= z) & (z > 0))
            def _():
                to_left(plane, source).wait_send()

            @pl.when(source != z)
            def _():
                for d in range(1, nt):
                    across(plane, source, t, lax.rem(t + d, nt)).wait_send()

    @pl.when(s < ns - 1)
    def _():
        halo(0).wait_send()

    @pl.when(s > 0)
    def _():
        halo(1).wait_send()

    for part in range(parts):
        @pl.loop(1, ns)
        def _(d):
            partial_to(part, lax.rem(s + d, ns)).wait_send()


def shards(test_modes, trial_modes, volumes):
    cell_count = trial_modes.shape[2] * trial_modes.shape[3] * trial_modes.shape[4]
    ns, nt, nz = lax.axis_size("space"), lax.axis_size("test"), lax.axis_size("trial")
    factor = 1.0 / (4.0 * math.sqrt(cell_count * ns))
    order = (2, 3, 0, 1, 4)
    own = jnp.transpose(trial_modes, order)
    weighted = jnp.transpose(
        (test_modes.astype(jnp.float32) * volumes).astype(jnp.bfloat16), order
    )
    planes, rows_each, _, modes, lanes = own.shape
    tests = weighted.shape[3]
    every = modes * nz
    piece = every // ns
    parts = tests // (GROUP * 4)
    width = tests * modes // parts
    dma = pltpu.SemaphoreType.DMA
    mine = pl.pallas_call(
        functools.partial(kernel, factor),
        out_shape=jax.ShapeDtypeStruct((piece, tests * modes), jnp.float32),
        in_specs=[pl.BlockSpec(memory_space=pltpu.VMEM)] * 2,
        out_specs=pl.BlockSpec(memory_space=pltpu.VMEM),
        scratch_shapes=[
            pltpu.VMEM((planes + 2, rows_each, 3, modes, lanes), jnp.bfloat16),
            pltpu.VMEM((planes, nz, rows_each, 3, modes, lanes), jnp.bfloat16),
            pltpu.VMEM(weighted.shape, jnp.float32),
            pltpu.VMEM((planes, rows_each, 3, 3, modes, lanes), MIXED),
            pltpu.VMEM((tests * modes, every), jnp.float32),
            pltpu.VMEM((parts, ns, piece, width), jnp.float32),
            pltpu.VMEM((parts, ns, piece, width), jnp.bfloat16),
            pltpu.VMEM((parts, ns, piece, width), jnp.bfloat16),
            dma((2,)),
            dma((2,)),
            dma((planes, nz)),
            dma((planes, nz)),
            dma((planes, nz)),
            dma((planes, nz, nt)),
            dma((planes, nz, nt)),
            dma((parts, ns)),
            dma((parts, ns)),
        ],
        compiler_params=pltpu.CompilerParams(
            vmem_limit_bytes=48 * 2**20, collective_id=0, has_side_effects=True
        ),
    )(own, weighted)
    return mine.reshape(piece, tests, modes)


def solution(mesh):
    return jax.shard_map(
        shards,
        mesh=mesh,
        in_specs=(
            P(None, "test", "space", None, None),
            P(None, "trial", "space", None, None),
            P("space", None, None),
        ),
        out_specs=P("space", "test", "trial"),
        check_vma=False,
    )
```

```python
import functools
import math

import jax
import jax.numpy as jnp
from jax import lax
from jax.experimental import pallas as pl
from jax.experimental.pallas import tpu as pltpu
from jax.sharding import PartitionSpec as P

GROUP = 8
MIXED = jnp.bfloat16
MESH = pl.DeviceIdType.MESH


def slope(later, earlier):
    return (later.astype(jnp.float32) - earlier.astype(jnp.float32)) * 0.5


def gradients_of_plane(before, here, after):
    rows, parts, modes, lanes = here.shape
    none = jnp.zeros((1, parts, modes, lanes), here.dtype)
    along_x = slope(after, before)
    along_y = slope(
        jnp.concatenate([here[1:], none], axis=0), jnp.concatenate([none, here[:-1]], axis=0)
    )
    wide = here.astype(jnp.float32).reshape(rows * parts * modes, lanes)
    lane = lax.broadcasted_iota(jnp.int32, wide.shape, 1)
    following = jnp.where(lane == lanes - 1, 0.0, pltpu.roll(wide, lanes - 1, 1))
    previous = jnp.where(lane == 0, 0.0, pltpu.roll(wide, 1, 1))
    along_z = ((following - previous) * 0.5).reshape(here.shape)
    return along_x, along_y, along_z


def spread(line, like):
    tile = jnp.broadcast_to(line, (16, line.shape[1])).astype(MIXED)
    return jnp.concatenate([tile] * (like.shape[0] // 16), axis=0)


def pair_rows(weighted_ref, grad_ref, plane, first_row, rows, first_mode):
    columns = []
    for row in range(rows):
        grads = [[grad_ref[plane, first_row + row, a, b] for b in range(3)] for a in range(3)]
        per_mode = []
        for mode in range(GROUP):
            w = [
                spread(weighted_ref[plane, first_row + row, a, pl.ds(first_mode + mode, 1), :], grads[0][0])
                for a in range(3)
            ]
            per_mode.append(
                [
                    (w[0] * grads[0][b] + w[1] * grads[1][b] + w[2] * grads[2][b]).astype(jnp.bfloat16)
                    for b in range(3)
                ]
            )
        for b in range(3):
            columns.append(jnp.concatenate([m[b] for m in per_mode], axis=0))
    return jnp.concatenate(columns, axis=1)


def kernel(
    factor, own_ref, test_ref, out_ref,
    padded_ref, all_ref, weighted_ref, grad_ref, total_ref, turned_ref, send_ref, got_ref,
    halo_send, halo_recv, right_send, left_send, line_recv, cross_send, cross_recv, sum_send, sum_recv,
):
    planes, rows_each, _, modes, lanes = own_ref.shape
    tests = weighted_ref.shape[3]
    s, t, z = lax.axis_index("space"), lax.axis_index("test"), lax.axis_index("trial")
    ns, nt, nz = lax.axis_size("space"), lax.axis_size("test"), lax.axis_size("trial")
    share = rows_each // nt
    pairs = rows_each // 2
    unroll = 4
    span = GROUP * unroll
    parts = tests // span
    every = out_ref.shape[0] * ns
    piece = out_ref.shape[0]

    def block(plane, source, part):
        return all_ref.at[plane, source, pl.ds(part * share, share)]

    def along_line(plane, source, target, sems):
        return pltpu.make_async_remote_copy(
            block(plane, source, t), block(plane, source, t),
            sems.at[plane, source], line_recv.at[plane, source],
            device_id=(s, t, target), device_id_type=MESH,
        )

    def to_right(plane, source):
        return along_line(plane, source, z + 1, right_send)

    def to_left(plane, source):
        return along_line(plane, source, z - 1, left_send)

    def across(plane, source, sender, target):
        return pltpu.make_async_remote_copy(
            block(plane, source, sender), block(plane, source, sender),
            cross_send.at[plane, source, target], cross_recv.at[plane, source, sender],
            device_id=(s, target, z), device_id_type=MESH,
        )

    def halo(side):
        return pltpu.make_async_remote_copy(
            padded_ref.at[planes if side == 0 else 1], padded_ref.at[0 if side == 0 else planes + 1],
            halo_send.at[side], halo_recv.at[side],
            device_id=(s + 1 if side == 0 else s - 1, t, z), device_id_type=MESH,
        )

    def partial_to(part, peer):
        return pltpu.make_async_remote_copy(
            send_ref.at[part, peer], got_ref.at[part, s],
            sum_send.at[part, peer], sum_recv.at[part, s],
            device_id=(peer, t, z), device_id_type=MESH,
        )

    def partial_from(part, peer):
        return pltpu.make_async_remote_copy(
            send_ref.at[part, peer], got_ref.at[part, peer],
            sum_send.at[part, peer], sum_recv.at[part, peer],
            device_id=(peer, t, z), device_id_type=MESH,
        )

    barrier = pltpu.get_barrier_semaphore()

    @pl.loop(1, ns)
    def _(d):
        pl.semaphore_signal(barrier, inc=1, device_id=(lax.rem(s + d, ns), t, z), device_id_type=MESH)

    for d in range(1, nt):
        pl.semaphore_signal(barrier, inc=1, device_id=(s, lax.rem(t + d, nt), z), device_id_type=MESH)

    @pl.when(z > 0)
    def _():
        pl.semaphore_signal(barrier, inc=1, device_id=(s, t, z - 1), device_id_type=MESH)

    @pl.when(z < nz - 1)
    def _():
        pl.semaphore_signal(barrier, inc=1, device_id=(s, t, z + 1), device_id_type=MESH)

    @pl.loop(0, planes)
    def _(plane):
        here = own_ref[plane]
        padded_ref[plane + 1] = here
        all_ref[plane, z] = here

    sides = jnp.where(z > 0, 1, 0) + jnp.where(z < nz - 1, 1, 0)
    pl.semaphore_wait(barrier, ns - 1 + nt - 1 + sides)

    def send_own(plane):
        @pl.when(z < nz - 1)
        def _():
            to_right(plane, z).start()

        @pl.when(z > 0)
        def _():
            to_left(plane, z).start()

    def pass_on(plane, hop):
        before, after = z - hop, z + hop

        @pl.when(before >= 0)
        def _():
            to_right(plane, before).wait_recv()

            @pl.when(z < nz - 1)
            def _():
                to_right(plane, before).start()

            for d in range(1, nt):
                across(plane, before, t, lax.rem(t + d, nt)).start()

        @pl.when(after < nz)
        def _():
            to_left(plane, after).wait_recv()

            @pl.when(z > 0)
            def _():
                to_left(plane, after).start()

            for d in range(1, nt):
                across(plane, after, t, lax.rem(t + d, nt)).start()

    def slot(plane, hop):
        @pl.when((hop == 0) & (plane + 1 < planes))
        def _():
            send_own(plane + 1)

        @pl.when(hop > 0)
        def _():
            pass_on(plane, hop)

    def wait_across(plane):
        for d in range(1, nz):
            source = lax.rem(z + d, nz)
            for e in range(1, nt):
                across(plane, source, lax.rem(t + e, nt), t).wait_recv()

    send_own(0)

    @pl.when(s < ns - 1)
    def _():
        halo(0).start()

    @pl.when(s > 0)
    def _():
        halo(1).start()

    slot(0, 0)

    @pl.when(s == 0)
    def _():
        padded_ref[0] = jnp.zeros(padded_ref.shape[1:], padded_ref.dtype)

    @pl.when(s == ns - 1)
    def _():
        padded_ref[planes + 1] = jnp.zeros(padded_ref.shape[1:], padded_ref.dtype)

    @pl.loop(0, planes)
    def _(plane):
        weighted_ref[plane] = test_ref[plane].astype(jnp.float32)

    total_ref[...] = jnp.zeros_like(total_ref)
    slot(0, 1)

    def find_gradients(plane):
        found = gradients_of_plane(padded_ref[plane], padded_ref[plane + 1], padded_ref[plane + 2])
        for b in range(3):
            grad_ref[plane, :, :, b] = found[b].astype(jnp.bfloat16).astype(MIXED)

    pl.loop(1, planes - 1)(find_gradients)

    @pl.when(s > 0)
    def _():
        halo(0).wait_recv()

    @pl.when(s < ns - 1)
    def _():
        halo(1).wait_recv()

    for hop in range(2, nz):
        slot(0, hop)
        if hop == 2:
            for plane in sorted({0, planes - 1}):
                find_gradients(plane)

    def flush(part):
        rows = span * modes
        value = total_ref[pl.ds(pl.multiple_of(part * rows, rows), rows), :].T
        for peer in range(ns):
            turned_ref[part, peer] = value[peer * piece : (peer + 1) * piece]
            send_ref[part, peer] = value[peer * piece : (peer + 1) * piece].astype(jnp.bfloat16)

        @pl.loop(1, ns)
        def _(d):
            partial_to(part, lax.rem(s + d, ns)).start()

    @pl.loop(0, planes * pairs * parts)
    def _(step):
        plane, m = step // (pairs * parts), step % (pairs * parts)
        last = plane == planes - 1
        early = pairs // nt
        late = m - early * parts
        by_part = last & (late >= 0)
        q = jnp.where(by_part, early + late % (pairs - early), m // parts)
        part = jnp.where(by_part, late // (pairs - early), m % parts)
        row = lax.rem(t * share + q * 2, rows_each)

        @pl.when(m == early * parts)
        def _():
            wait_across(plane)

        trial = jnp.concatenate(
            [
                jnp.concatenate([all_ref[plane, source, row + r, b] for source in range(nz)], axis=0)
                for r in range(2)
                for b in range(3)
            ],
            axis=1,
        )
        for u in range(unroll):
            first = part * span + u * GROUP
            lhs = pair_rows(weighted_ref, grad_ref, plane, row, 2, first)
            where = pl.ds(pl.multiple_of(first * modes, GROUP * modes), GROUP * modes)
            total_ref[where, :] += lax.dot_general(
                lhs, trial, (((1,), (1,)), ((), ())), preferred_element_type=jnp.float32
            )

        @pl.when((plane + 1 < planes) & (m % parts == parts - 1))
        def _():
            @pl.loop(m // parts * nz // pairs, (m // parts + 1) * nz // pairs)
            def _(hop):
                slot(plane + 1, hop)

        @pl.when(by_part & (late % (pairs - early) == pairs - early - 1))
        def _():
            flush(part)

    width = span * modes
    for part in range(parts):
        @pl.loop(1, ns)
        def _(d):
            peer = lax.rem(s + d, ns)
            partial_from(part, peer).wait_recv()
            turned_ref[part, s] += got_ref[part, peer].astype(jnp.float32)

        out_ref[:, part * width : (part + 1) * width] = turned_ref[part, s] * factor

    @pl.loop(0, planes)
    def _(plane):
        @pl.loop(0, nz)
        def _(source):
            @pl.when((source <= z) & (z < nz - 1))
            def _():
                to_right(plane, source).wait_send()

            @pl.when((source >= z) & (z > 0))
            def _():
                to_left(plane, source).wait_send()

            @pl.when(source != z)
            def _():
                for d in range(1, nt):
                    across(plane, source, t, lax.rem(t + d, nt)).wait_send()

    @pl.when(s < ns - 1)
    def _():
        halo(0).wait_send()

    @pl.when(s > 0)
    def _():
        halo(1).wait_send()

    for part in range(parts):
        @pl.loop(1, ns)
        def _(d):
            partial_to(part, lax.rem(s + d, ns)).wait_send()


def shards(test_modes, trial_modes, volumes):
    cell_count = trial_modes.shape[2] * trial_modes.shape[3] * trial_modes.shape[4]
    ns, nt, nz = lax.axis_size("space"), lax.axis_size("test"), lax.axis_size("trial")
    factor = 1.0 / (4.0 * math.sqrt(cell_count * ns))
    order = (2, 3, 0, 1, 4)
    own = jnp.transpose(trial_modes, order)
    weighted = jnp.transpose(
        (test_modes.astype(jnp.float32) * volumes).astype(jnp.bfloat16), order
    )
    planes, rows_each, _, modes, lanes = own.shape
    tests = weighted.shape[3]
    every = modes * nz
    piece = every // ns
    parts = tests // (GROUP * 4)
    width = tests * modes // parts
    dma = pltpu.SemaphoreType.DMA
    mine = pl.pallas_call(
        functools.partial(kernel, factor),
        out_shape=jax.ShapeDtypeStruct((piece, tests * modes), jnp.float32),
        in_specs=[pl.BlockSpec(memory_space=pltpu.VMEM)] * 2,
        out_specs=pl.BlockSpec(memory_space=pltpu.VMEM),
        scratch_shapes=[
            pltpu.VMEM((planes + 2, rows_each, 3, modes, lanes), jnp.bfloat16),
            pltpu.VMEM((planes, nz, rows_each, 3, modes, lanes), jnp.bfloat16),
            pltpu.VMEM(weighted.shape, jnp.float32),
            pltpu.VMEM((planes, rows_each, 3, 3, modes, lanes), MIXED),
            pltpu.VMEM((tests * modes, every), jnp.float32),
            pltpu.VMEM((parts, ns, piece, width), jnp.float32),
            pltpu.VMEM((parts, ns, piece, width), jnp.bfloat16),
            pltpu.VMEM((parts, ns, piece, width), jnp.bfloat16),
            dma((2,)),
            dma((2,)),
            dma((planes, nz)),
            dma((planes, nz)),
            dma((planes, nz)),
            dma((planes, nz, nt)),
            dma((planes, nz, nt)),
            dma((parts, ns)),
            dma((parts, ns)),
        ],
        compiler_params=pltpu.CompilerParams(
            vmem_limit_bytes=48 * 2**20, collective_id=0, has_side_effects=True
        ),
    )(own, weighted)
    return mine.reshape(piece, tests, modes)


def solution(mesh):
    return jax.shard_map(
        shards,
        mesh=mesh,
        in_specs=(
            P(None, "test", "space", None, None),
            P(None, "trial", "space", None, None),
            P("space", None, None),
        ),
        out_specs=P("space", "test", "trial"),
        check_vma=False,
    )
```

```python
import functools
import math

import jax
import jax.numpy as jnp
from jax import lax
from jax.experimental import pallas as pl
from jax.experimental.pallas import tpu as pltpu
from jax.sharding import PartitionSpec as P

GROUP = 8
MIXED = jnp.bfloat16
MESH = pl.DeviceIdType.MESH


def slope(later, earlier):
    return (later.astype(jnp.float32) - earlier.astype(jnp.float32)) * 0.5


def gradients_of_plane(before, here, after):
    rows, parts, modes, lanes = here.shape
    none = jnp.zeros((1, parts, modes, lanes), here.dtype)
    along_x = slope(after, before)
    along_y = slope(
        jnp.concatenate([here[1:], none], axis=0), jnp.concatenate([none, here[:-1]], axis=0)
    )
    wide = here.astype(jnp.float32).reshape(rows * parts * modes, lanes)
    lane = lax.broadcasted_iota(jnp.int32, wide.shape, 1)
    following = jnp.where(lane == lanes - 1, 0.0, pltpu.roll(wide, lanes - 1, 1))
    previous = jnp.where(lane == 0, 0.0, pltpu.roll(wide, 1, 1))
    along_z = ((following - previous) * 0.5).reshape(here.shape)
    return along_x, along_y, along_z


def spread(line, like):
    tile = jnp.broadcast_to(line, (16, line.shape[1])).astype(MIXED)
    return jnp.concatenate([tile] * (like.shape[0] // 16), axis=0)


def pair_rows(weighted_ref, grad_ref, plane, first_row, rows, first_mode):
    columns = []
    for row in range(rows):
        grads = [[grad_ref[plane, first_row + row, a, b] for b in range(3)] for a in range(3)]
        per_mode = []
        for mode in range(GROUP):
            w = [
                spread(weighted_ref[plane, first_row + row, a, pl.ds(first_mode + mode, 1), :], grads[0][0])
                for a in range(3)
            ]
            per_mode.append(
                [
                    (w[0] * grads[0][b] + w[1] * grads[1][b] + w[2] * grads[2][b]).astype(jnp.bfloat16)
                    for b in range(3)
                ]
            )
        for b in range(3):
            columns.append(jnp.concatenate([m[b] for m in per_mode], axis=0))
    return jnp.concatenate(columns, axis=1)


def kernel(
    factor, own_ref, test_ref, out_ref,
    padded_ref, all_ref, weighted_ref, grad_ref, total_ref, turned_ref, send_ref, got_ref,
    halo_send, halo_recv, right_send, left_send, line_recv, cross_send, cross_recv, sum_send, sum_recv,
):
    planes, rows_each, _, modes, lanes = own_ref.shape
    tests = weighted_ref.shape[3]
    s, t, z = lax.axis_index("space"), lax.axis_index("test"), lax.axis_index("trial")
    ns, nt, nz = lax.axis_size("space"), lax.axis_size("test"), lax.axis_size("trial")
    chunks, deep = all_ref.shape[0], all_ref.shape[2]
    per_plane = chunks // planes
    share = deep // nt
    pairs = deep // 2
    unroll = 4
    span = GROUP * unroll
    parts = tests // span
    every = out_ref.shape[0] * ns
    piece = out_ref.shape[0]

    def block(chunk, source, part):
        return all_ref.at[chunk, source, pl.ds(part * share, share)]

    def along_line(plane, source, target, sems):
        return pltpu.make_async_remote_copy(
            block(plane, source, t), block(plane, source, t),
            sems.at[plane, source], line_recv.at[plane, source],
            device_id=(s, t, target), device_id_type=MESH,
        )

    def to_right(plane, source):
        return along_line(plane, source, z + 1, right_send)

    def to_left(plane, source):
        return along_line(plane, source, z - 1, left_send)

    def across(plane, source, sender, target):
        return pltpu.make_async_remote_copy(
            block(plane, source, sender), block(plane, source, sender),
            cross_send.at[plane, source, target], cross_recv.at[plane, source, sender],
            device_id=(s, target, z), device_id_type=MESH,
        )

    def halo(side):
        return pltpu.make_async_remote_copy(
            padded_ref.at[planes if side == 0 else 1], padded_ref.at[0 if side == 0 else planes + 1],
            halo_send.at[side], halo_recv.at[side],
            device_id=(s + 1 if side == 0 else s - 1, t, z), device_id_type=MESH,
        )

    def partial_to(part, peer):
        return pltpu.make_async_remote_copy(
            send_ref.at[part, peer], got_ref.at[part, s],
            sum_send.at[part, peer], sum_recv.at[part, s],
            device_id=(peer, t, z), device_id_type=MESH,
        )

    def partial_from(part, peer):
        return pltpu.make_async_remote_copy(
            send_ref.at[part, peer], got_ref.at[part, peer],
            sum_send.at[part, peer], sum_recv.at[part, peer],
            device_id=(peer, t, z), device_id_type=MESH,
        )

    barrier = pltpu.get_barrier_semaphore()

    @pl.loop(1, ns)
    def _(d):
        pl.semaphore_signal(barrier, inc=1, device_id=(lax.rem(s + d, ns), t, z), device_id_type=MESH)

    for d in range(1, nt):
        pl.semaphore_signal(barrier, inc=1, device_id=(s, lax.rem(t + d, nt), z), device_id_type=MESH)

    @pl.when(z > 0)
    def _():
        pl.semaphore_signal(barrier, inc=1, device_id=(s, t, z - 1), device_id_type=MESH)

    @pl.when(z < nz - 1)
    def _():
        pl.semaphore_signal(barrier, inc=1, device_id=(s, t, z + 1), device_id_type=MESH)

    @pl.loop(0, planes)
    def _(plane):
        here = own_ref[plane]
        padded_ref[plane + 1] = here
        for h in range(per_plane):
            all_ref[plane * per_plane + h, z] = here[h * deep : (h + 1) * deep]

    sides = jnp.where(z > 0, 1, 0) + jnp.where(z < nz - 1, 1, 0)
    pl.semaphore_wait(barrier, ns - 1 + nt - 1 + sides)

    def send_own(plane):
        @pl.when(z < nz - 1)
        def _():
            to_right(plane, z).start()

        @pl.when(z > 0)
        def _():
            to_left(plane, z).start()

    def pass_on(plane, hop):
        before, after = z - hop, z + hop

        @pl.when(before >= 0)
        def _():
            to_right(plane, before).wait_recv()

            @pl.when(z < nz - 1)
            def _():
                to_right(plane, before).start()

            for d in range(1, nt):
                across(plane, before, t, lax.rem(t + d, nt)).start()

        @pl.when(after < nz)
        def _():
            to_left(plane, after).wait_recv()

            @pl.when(z > 0)
            def _():
                to_left(plane, after).start()

            for d in range(1, nt):
                across(plane, after, t, lax.rem(t + d, nt)).start()

    def slot(plane, hop):
        @pl.when(hop > 0)
        def _():
            pass_on(plane, hop)

        @pl.when((hop == 1) & (plane + 2 < chunks))
        def _():
            send_own(plane + 2)

    def wait_across(plane):
        for d in range(1, nz):
            source = lax.rem(z + d, nz)
            for e in range(1, nt):
                across(plane, source, lax.rem(t + e, nt), t).wait_recv()

    send_own(0)
    send_own(1)

    @pl.when(s < ns - 1)
    def _():
        halo(0).start()

    @pl.when(s > 0)
    def _():
        halo(1).start()

    @pl.when(s == 0)
    def _():
        padded_ref[0] = jnp.zeros(padded_ref.shape[1:], padded_ref.dtype)

    @pl.when(s == ns - 1)
    def _():
        padded_ref[planes + 1] = jnp.zeros(padded_ref.shape[1:], padded_ref.dtype)

    @pl.loop(0, planes)
    def _(plane):
        weighted_ref[plane] = test_ref[plane].astype(jnp.float32)

    total_ref[...] = jnp.zeros_like(total_ref)
    slot(0, 1)

    def find_gradients(plane):
        found = gradients_of_plane(padded_ref[plane], padded_ref[plane + 1], padded_ref[plane + 2])
        for b in range(3):
            grad_ref[plane, :, :, b] = found[b].astype(jnp.bfloat16).astype(MIXED)

    pl.loop(1, planes - 1)(find_gradients)

    @pl.when(s > 0)
    def _():
        halo(0).wait_recv()

    @pl.when(s < ns - 1)
    def _():
        halo(1).wait_recv()

    for hop in range(2, nz):
        slot(0, hop)
        if hop == 2:
            for plane in sorted({0, planes - 1}):
                find_gradients(plane)

    def flush(part):
        rows = span * modes
        value = total_ref[pl.ds(pl.multiple_of(part * rows, rows), rows), :].T
        for peer in range(ns):
            turned_ref[part, peer] = value[peer * piece : (peer + 1) * piece]
            send_ref[part, peer] = value[peer * piece : (peer + 1) * piece].astype(jnp.bfloat16)

        @pl.loop(1, ns)
        def _(d):
            partial_to(part, lax.rem(s + d, ns)).start()

    @pl.loop(0, chunks * pairs * parts)
    def _(step):
        chunk, m = step // (pairs * parts), step % (pairs * parts)
        plane = chunk // per_plane
        last = chunk == chunks - 1
        early = pairs // nt
        late = m - early * parts
        by_part = last & (late >= 0)
        q = jnp.where(by_part, early + late % (pairs - early), m // parts)
        part = jnp.where(by_part, late // (pairs - early), m % parts)
        row = lax.rem(t * share + q * 2, deep)
        top = (chunk % per_plane) * deep + row

        @pl.when(m == early * parts)
        def _():
            wait_across(chunk)

        trial = jnp.concatenate(
            [
                jnp.concatenate([all_ref[chunk, source, row + r, b] for source in range(nz)], axis=0)
                for r in range(2)
                for b in range(3)
            ],
            axis=1,
        )
        for u in range(unroll):
            first = part * span + u * GROUP
            lhs = pair_rows(weighted_ref, grad_ref, plane, top, 2, first)
            where = pl.ds(pl.multiple_of(first * modes, GROUP * modes), GROUP * modes)
            total_ref[where, :] += lax.dot_general(
                lhs, trial, (((1,), (1,)), ((), ())), preferred_element_type=jnp.float32
            )

        @pl.when(chunk + 1 < chunks)
        def _():
            @pl.loop(m * nz // (pairs * parts), (m + 1) * nz // (pairs * parts))
            def _(hop):
                slot(chunk + 1, hop)

        @pl.when(by_part & (late % (pairs - early) == pairs - early - 1))
        def _():
            flush(part)

    width = span * modes
    for part in range(parts):
        @pl.loop(1, ns)
        def _(d):
            peer = lax.rem(s + d, ns)
            partial_from(part, peer).wait_recv()
            turned_ref[part, s] += got_ref[part, peer].astype(jnp.float32)

        out_ref[:, part * width : (part + 1) * width] = turned_ref[part, s] * factor

    @pl.loop(0, chunks)
    def _(plane):
        @pl.loop(0, nz)
        def _(source):
            @pl.when((source <= z) & (z < nz - 1))
            def _():
                to_right(plane, source).wait_send()

            @pl.when((source >= z) & (z > 0))
            def _():
                to_left(plane, source).wait_send()

            @pl.when(source != z)
            def _():
                for d in range(1, nt):
                    across(plane, source, t, lax.rem(t + d, nt)).wait_send()

    @pl.when(s < ns - 1)
    def _():
        halo(0).wait_send()

    @pl.when(s > 0)
    def _():
        halo(1).wait_send()

    for part in range(parts):
        @pl.loop(1, ns)
        def _(d):
            partial_to(part, lax.rem(s + d, ns)).wait_send()


def shards(test_modes, trial_modes, volumes):
    cell_count = trial_modes.shape[2] * trial_modes.shape[3] * trial_modes.shape[4]
    ns, nt, nz = lax.axis_size("space"), lax.axis_size("test"), lax.axis_size("trial")
    factor = 1.0 / (4.0 * math.sqrt(cell_count * ns))
    order = (2, 3, 0, 1, 4)
    own = jnp.transpose(trial_modes, order)
    weighted = jnp.transpose(
        (test_modes.astype(jnp.float32) * volumes).astype(jnp.bfloat16), order
    )
    planes, rows_each, _, modes, lanes = own.shape
    tests = weighted.shape[3]
    every = modes * nz
    piece = every // ns
    parts = tests // (GROUP * 4)
    width = tests * modes // parts
    halves = 2
    chunks = planes * halves
    dma = pltpu.SemaphoreType.DMA
    mine = pl.pallas_call(
        functools.partial(kernel, factor),
        out_shape=jax.ShapeDtypeStruct((piece, tests * modes), jnp.float32),
        in_specs=[pl.BlockSpec(memory_space=pltpu.VMEM)] * 2,
        out_specs=pl.BlockSpec(memory_space=pltpu.VMEM),
        scratch_shapes=[
            pltpu.VMEM((planes + 2, rows_each, 3, modes, lanes), jnp.bfloat16),
            pltpu.VMEM((chunks, nz, rows_each // halves, 3, modes, lanes), jnp.bfloat16),
            pltpu.VMEM(weighted.shape, jnp.float32),
            pltpu.VMEM((planes, rows_each, 3, 3, modes, lanes), MIXED),
            pltpu.VMEM((tests * modes, every), jnp.float32),
            pltpu.VMEM((parts, ns, piece, width), jnp.float32),
            pltpu.VMEM((parts, ns, piece, width), jnp.bfloat16),
            pltpu.VMEM((parts, ns, piece, width), jnp.bfloat16),
            dma((2,)),
            dma((2,)),
            dma((chunks, nz)),
            dma((chunks, nz)),
            dma((chunks, nz)),
            dma((chunks, nz, nt)),
            dma((chunks, nz, nt)),
            dma((parts, ns)),
            dma((parts, ns)),
        ],
        compiler_params=pltpu.CompilerParams(
            vmem_limit_bytes=48 * 2**20, collective_id=0, has_side_effects=True
        ),
    )(own, weighted)
    return mine.reshape(piece, tests, modes)


def solution(mesh):
    return jax.shard_map(
        shards,
        mesh=mesh,
        in_specs=(
            P(None, "test", "space", None, None),
            P(None, "trial", "space", None, None),
            P("space", None, None),
        ),
        out_specs=P("space", "test", "trial"),
        check_vma=False,
    )
```

```python
import functools
import math

import jax
import jax.numpy as jnp
from jax import lax
from jax.experimental import pallas as pl
from jax.experimental.pallas import tpu as pltpu
from jax.sharding import PartitionSpec as P

GROUP = 8
MIXED = jnp.bfloat16
MESH = pl.DeviceIdType.MESH


def slope(later, earlier):
    return (later.astype(jnp.float32) - earlier.astype(jnp.float32)) * 0.5


def gradients_of_plane(before, here, after):
    rows, parts, modes, lanes = here.shape
    none = jnp.zeros((1, parts, modes, lanes), here.dtype)
    along_x = slope(after, before)
    along_y = slope(
        jnp.concatenate([here[1:], none], axis=0), jnp.concatenate([none, here[:-1]], axis=0)
    )
    wide = here.astype(jnp.float32).reshape(rows * parts * modes, lanes)
    lane = lax.broadcasted_iota(jnp.int32, wide.shape, 1)
    following = jnp.where(lane == lanes - 1, 0.0, pltpu.roll(wide, lanes - 1, 1))
    previous = jnp.where(lane == 0, 0.0, pltpu.roll(wide, 1, 1))
    along_z = ((following - previous) * 0.5).reshape(here.shape)
    return along_x, along_y, along_z


def spread(line, like):
    tile = jnp.broadcast_to(line, (16, line.shape[1])).astype(MIXED)
    return jnp.concatenate([tile] * (like.shape[0] // 16), axis=0)


def pair_rows(weighted_ref, grad_ref, plane, first_row, rows, first_mode):
    columns = []
    for row in range(rows):
        grads = [[grad_ref[plane, first_row + row, a, b] for b in range(3)] for a in range(3)]
        per_mode = []
        for mode in range(GROUP):
            w = [
                spread(weighted_ref[plane, first_row + row, a, pl.ds(first_mode + mode, 1), :], grads[0][0])
                for a in range(3)
            ]
            per_mode.append(
                [
                    (w[0] * grads[0][b] + w[1] * grads[1][b] + w[2] * grads[2][b]).astype(jnp.bfloat16)
                    for b in range(3)
                ]
            )
        for b in range(3):
            columns.append(jnp.concatenate([m[b] for m in per_mode], axis=0))
    return jnp.concatenate(columns, axis=1)


def kernel(
    factor, own_ref, test_ref, out_ref,
    padded_ref, all_ref, weighted_ref, grad_ref, total_ref, turned_ref, send_ref, got_ref,
    halo_send, halo_recv, right_send, left_send, line_recv, cross_send, cross_recv, sum_send, sum_recv,
):
    planes, rows_each, _, modes, lanes = own_ref.shape
    tests = weighted_ref.shape[3]
    s, t, z = lax.axis_index("space"), lax.axis_index("test"), lax.axis_index("trial")
    ns, nt, nz = lax.axis_size("space"), lax.axis_size("test"), lax.axis_size("trial")
    chunks, deep = all_ref.shape[0], all_ref.shape[2]
    per_plane = chunks // planes
    share = deep // nt
    pairs = deep // 2
    unroll = 4
    span = GROUP * unroll
    parts = tests // span
    every = out_ref.shape[0] * ns
    piece = out_ref.shape[0]

    def block(chunk, source, part):
        return all_ref.at[chunk, source, pl.ds(part * share, share)]

    def along_line(plane, source, target, sems):
        return pltpu.make_async_remote_copy(
            block(plane, source, t), block(plane, source, t),
            sems.at[plane, source], line_recv.at[plane, source],
            device_id=(s, t, target), device_id_type=MESH,
        )

    def to_right(plane, source):
        return along_line(plane, source, z + 1, right_send)

    def to_left(plane, source):
        return along_line(plane, source, z - 1, left_send)

    def across(plane, source, sender, target):
        return pltpu.make_async_remote_copy(
            block(plane, source, sender), block(plane, source, sender),
            cross_send.at[plane, source, target], cross_recv.at[plane, source, sender],
            device_id=(s, target, z), device_id_type=MESH,
        )

    def halo(side):
        return pltpu.make_async_remote_copy(
            padded_ref.at[planes if side == 0 else 1], padded_ref.at[0 if side == 0 else planes + 1],
            halo_send.at[side], halo_recv.at[side],
            device_id=(s + 1 if side == 0 else s - 1, t, z), device_id_type=MESH,
        )

    def partial_to(part, peer):
        return pltpu.make_async_remote_copy(
            send_ref.at[part, peer], got_ref.at[part, s],
            sum_send.at[part, peer], sum_recv.at[part, s],
            device_id=(peer, t, z), device_id_type=MESH,
        )

    def partial_from(part, peer):
        return pltpu.make_async_remote_copy(
            send_ref.at[part, peer], got_ref.at[part, peer],
            sum_send.at[part, peer], sum_recv.at[part, peer],
            device_id=(peer, t, z), device_id_type=MESH,
        )

    barrier = pltpu.get_barrier_semaphore()

    @pl.loop(1, ns)
    def _(d):
        pl.semaphore_signal(barrier, inc=1, device_id=(lax.rem(s + d, ns), t, z), device_id_type=MESH)

    for d in range(1, nt):
        pl.semaphore_signal(barrier, inc=1, device_id=(s, lax.rem(t + d, nt), z), device_id_type=MESH)

    @pl.when(z > 0)
    def _():
        pl.semaphore_signal(barrier, inc=1, device_id=(s, t, z - 1), device_id_type=MESH)

    @pl.when(z < nz - 1)
    def _():
        pl.semaphore_signal(barrier, inc=1, device_id=(s, t, z + 1), device_id_type=MESH)

    @pl.loop(0, planes)
    def _(plane):
        here = own_ref[plane]
        padded_ref[plane + 1] = here
        for h in range(per_plane):
            all_ref[plane * per_plane + h, z] = here[h * deep : (h + 1) * deep]

    sides = jnp.where(z > 0, 1, 0) + jnp.where(z < nz - 1, 1, 0)
    pl.semaphore_wait(barrier, ns - 1 + nt - 1 + sides)

    def send_own(plane):
        @pl.when(z < nz - 1)
        def _():
            to_right(plane, z).start()

        @pl.when(z > 0)
        def _():
            to_left(plane, z).start()

    def pass_on(plane, hop):
        before, after = z - hop, z + hop

        @pl.when(before >= 0)
        def _():
            to_right(plane, before).wait_recv()

            @pl.when(z < nz - 1)
            def _():
                to_right(plane, before).start()

            for d in range(1, nt):
                across(plane, before, t, lax.rem(t + d, nt)).start()

        @pl.when(after < nz)
        def _():
            to_left(plane, after).wait_recv()

            @pl.when(z > 0)
            def _():
                to_left(plane, after).start()

            for d in range(1, nt):
                across(plane, after, t, lax.rem(t + d, nt)).start()

    def slot(stage, hop):
        chunk = stage - hop + 1

        @pl.when((hop > 0) & (chunk >= 0) & (chunk < chunks))
        def _():
            pass_on(chunk, hop)

        @pl.when((hop == 1) & (stage + 2 < chunks))
        def _():
            send_own(stage + 2)

    def wait_across(plane):
        for d in range(1, nz):
            source = lax.rem(z + d, nz)
            for e in range(1, nt):
                across(plane, source, lax.rem(t + e, nt), t).wait_recv()

    send_own(0)
    send_own(1)

    @pl.when(s < ns - 1)
    def _():
        halo(0).start()

    @pl.when(s > 0)
    def _():
        halo(1).start()

    @pl.when(s == 0)
    def _():
        padded_ref[0] = jnp.zeros(padded_ref.shape[1:], padded_ref.dtype)

    @pl.when(s == ns - 1)
    def _():
        padded_ref[planes + 1] = jnp.zeros(padded_ref.shape[1:], padded_ref.dtype)

    @pl.loop(0, planes)
    def _(plane):
        weighted_ref[plane] = test_ref[plane].astype(jnp.float32)

    total_ref[...] = jnp.zeros_like(total_ref)
    slot(0, 1)

    def find_gradients(plane):
        found = gradients_of_plane(padded_ref[plane], padded_ref[plane + 1], padded_ref[plane + 2])
        for b in range(3):
            grad_ref[plane, :, :, b] = found[b].astype(jnp.bfloat16).astype(MIXED)

    pl.loop(1, planes - 1)(find_gradients)

    @pl.when(s > 0)
    def _():
        halo(0).wait_recv()

    @pl.when(s < ns - 1)
    def _():
        halo(1).wait_recv()

    for stage in range(1, nz - 1):
        for hop in range(min(stage + 1, nz - 1), 0, -1):
            slot(stage, hop)
        if stage == 1:
            for plane in sorted({0, planes - 1}):
                find_gradients(plane)

    def flush(part):
        rows = span * modes
        value = total_ref[pl.ds(pl.multiple_of(part * rows, rows), rows), :].T
        for peer in range(ns):
            turned_ref[part, peer] = value[peer * piece : (peer + 1) * piece]
            send_ref[part, peer] = value[peer * piece : (peer + 1) * piece].astype(jnp.bfloat16)

        @pl.loop(1, ns)
        def _(d):
            partial_to(part, lax.rem(s + d, ns)).start()

    @pl.loop(0, chunks * pairs * parts)
    def _(step):
        chunk, m = step // (pairs * parts), step % (pairs * parts)
        plane = chunk // per_plane
        last = chunk == chunks - 1
        early = pairs // nt
        late = m - early * parts
        by_part = last & (late >= 0)
        q = jnp.where(by_part, early + late % (pairs - early), m // parts)
        part = jnp.where(by_part, late // (pairs - early), m % parts)
        row = lax.rem(t * share + q * 2, deep)
        top = (chunk % per_plane) * deep + row

        @pl.when(m == early * parts)
        def _():
            wait_across(chunk)

        trial = jnp.concatenate(
            [
                jnp.concatenate([all_ref[chunk, source, row + r, b] for source in range(nz)], axis=0)
                for r in range(2)
                for b in range(3)
            ],
            axis=1,
        )
        for u in range(unroll):
            first = part * span + u * GROUP
            lhs = pair_rows(weighted_ref, grad_ref, plane, top, 2, first)
            where = pl.ds(pl.multiple_of(first * modes, GROUP * modes), GROUP * modes)
            total_ref[where, :] += lax.dot_general(
                lhs, trial, (((1,), (1,)), ((), ())), preferred_element_type=jnp.float32
            )

        @pl.loop(m * nz // (pairs * parts), (m + 1) * nz // (pairs * parts))
        def _(turn):
            slot(chunk + nz - 1, nz - 1 - turn)

        @pl.when(by_part & (late % (pairs - early) == pairs - early - 1))
        def _():
            flush(part)

    width = span * modes
    for part in range(parts):
        @pl.loop(1, ns)
        def _(d):
            peer = lax.rem(s + d, ns)
            partial_from(part, peer).wait_recv()
            turned_ref[part, s] += got_ref[part, peer].astype(jnp.float32)

        out_ref[:, part * width : (part + 1) * width] = turned_ref[part, s] * factor

    @pl.loop(0, chunks)
    def _(plane):
        @pl.loop(0, nz)
        def _(source):
            @pl.when((source <= z) & (z < nz - 1))
            def _():
                to_right(plane, source).wait_send()

            @pl.when((source >= z) & (z > 0))
            def _():
                to_left(plane, source).wait_send()

            @pl.when(source != z)
            def _():
                for d in range(1, nt):
                    across(plane, source, t, lax.rem(t + d, nt)).wait_send()

    @pl.when(s < ns - 1)
    def _():
        halo(0).wait_send()

    @pl.when(s > 0)
    def _():
        halo(1).wait_send()

    for part in range(parts):
        @pl.loop(1, ns)
        def _(d):
            partial_to(part, lax.rem(s + d, ns)).wait_send()


def shards(test_modes, trial_modes, volumes):
    cell_count = trial_modes.shape[2] * trial_modes.shape[3] * trial_modes.shape[4]
    ns, nt, nz = lax.axis_size("space"), lax.axis_size("test"), lax.axis_size("trial")
    factor = 1.0 / (4.0 * math.sqrt(cell_count * ns))
    order = (2, 3, 0, 1, 4)
    own = jnp.transpose(trial_modes, order)
    weighted = jnp.transpose(
        (test_modes.astype(jnp.float32) * volumes).astype(jnp.bfloat16), order
    )
    planes, rows_each, _, modes, lanes = own.shape
    tests = weighted.shape[3]
    every = modes * nz
    piece = every // ns
    parts = tests // (GROUP * 4)
    width = tests * modes // parts
    halves = 2
    chunks = planes * halves
    dma = pltpu.SemaphoreType.DMA
    mine = pl.pallas_call(
        functools.partial(kernel, factor),
        out_shape=jax.ShapeDtypeStruct((piece, tests * modes), jnp.float32),
        in_specs=[pl.BlockSpec(memory_space=pltpu.VMEM)] * 2,
        out_specs=pl.BlockSpec(memory_space=pltpu.VMEM),
        scratch_shapes=[
            pltpu.VMEM((planes + 2, rows_each, 3, modes, lanes), jnp.bfloat16),
            pltpu.VMEM((chunks, nz, rows_each // halves, 3, modes, lanes), jnp.bfloat16),
            pltpu.VMEM(weighted.shape, jnp.float32),
            pltpu.VMEM((planes, rows_each, 3, 3, modes, lanes), MIXED),
            pltpu.VMEM((tests * modes, every), jnp.float32),
            pltpu.VMEM((parts, ns, piece, width), jnp.float32),
            pltpu.VMEM((parts, ns, piece, width), jnp.bfloat16),
            pltpu.VMEM((parts, ns, piece, width), jnp.bfloat16),
            dma((2,)),
            dma((2,)),
            dma((chunks, nz)),
            dma((chunks, nz)),
            dma((chunks, nz)),
            dma((chunks, nz, nt)),
            dma((chunks, nz, nt)),
            dma((parts, ns)),
            dma((parts, ns)),
        ],
        compiler_params=pltpu.CompilerParams(
            vmem_limit_bytes=48 * 2**20, collective_id=0, has_side_effects=True
        ),
    )(own, weighted)
    return mine.reshape(piece, tests, modes)


def solution(mesh):
    return jax.shard_map(
        shards,
        mesh=mesh,
        in_specs=(
            P(None, "test", "space", None, None),
            P(None, "trial", "space", None, None),
            P("space", None, None),
        ),
        out_specs=P("space", "test", "trial"),
        check_vma=False,
    )
```
